512 devices in a mesh: seq: 64 (over z, y), head: 8 (over x, core).
Axes of the slice: x: 4, y: 4, z: 16, core: 2. Of those that a mesh axis runs over, the one named last changes fastest.
Arguments:
- queries: bfloat16 [81920, 2048], P('seq', 'head'), may hold values from -6 to 6
- keys: bfloat16 [81920, 2048], P('seq', 'head'), may hold values from -6 to 6
- values: bfloat16 [81920, 2048], P('seq', 'head'), may hold values from -6 to 6
- grad_out: bfloat16 [81920, 2048], P('seq', 'head'), may hold values from -6 to 6
Outputs:
- attended: bfloat16 [81920, 2048], P('seq', 'head')
- grad_queries: bfloat16 [81920, 2048], P('seq', 'head')
- grad_keys: bfloat16 [81920, 2048], P('seq', 'head')
- grad_values: bfloat16 [81920, 2048], P('seq', 'head')
The draws below stay inside these ranges and needn't reach their ends.
All inputs are finite; a program needn't handle non-finite values.
Results may differ from the reference program's by a relative error of at most 0.0049.
Values sent between devices are 32-bit elements; how exact they have to be, the bound alone decides.
A program may use at most 64 MiB of HBM per device.

```python
import jax
import jax.numpy as jnp
from jax import lax

HEADS = 16
DH = 128
GROUP = 256
TOKENS = 81920


def block_levels(key, shape, shards, low, top_value):
    gain = 1.0
    for dim, shards_of in shards:
        draws = jax.random.uniform(jax.random.fold_in(jax.random.fold_in(key, 6), dim), (shards_of,), jnp.float32, low / len(shards), top_value / len(shards))
        gain = gain * jnp.repeat(jnp.exp(draws), shape[dim] // shards_of).reshape((-1,) + (1,) * (len(shape) - 1 - dim))
    return gain


def gaussian(rng, extent, deviation, most, shards=(), held_as=jnp.bfloat16):
    entries = jax.random.normal(rng, extent, jnp.float32) * deviation
    if len(shards) > 0:
        entries = block_levels(rng, extent, shards, -0.22, 0.18) * entries
    return jnp.clip(entries, min=-most, max=most).astype(held_as)


def setup_inputs(seed: int = 0) -> dict:
    arg_keys = jax.random.split(jax.random.key(seed), 5)
    queries = gaussian(arg_keys[0], (TOKENS, HEADS * DH), 1.0, 6.0, ((0, 64), (1, 8)))
    keys = gaussian(arg_keys[1], (TOKENS, HEADS * DH), 1.0, 6.0, ((0, 64), (1, 8)))
    values = gaussian(arg_keys[2], (TOKENS, HEADS * DH), 1.0, 6.0, ((0, 64), (1, 8)))
    grad_out = gaussian(arg_keys[3], (TOKENS, HEADS * DH), 1.0, 6.0, ((0, 64), (1, 8)))
    return {"queries": queries, "keys": keys, "values": values, "grad_out": grad_out}


def one_head(pieces):
    query, key, value, cotangent = pieces
    blocks = query.shape[0] // GROUP
    scale = (DH * TOKENS) ** -0.5
    qc = query.reshape(blocks, GROUP, DH).astype(jnp.float32)
    kc = key.reshape(blocks, GROUP, DH).astype(jnp.float32)
    vc = value.reshape(blocks, GROUP, DH).astype(jnp.float32)
    gc = cotangent.reshape(blocks, GROUP, DH).astype(jnp.float32)
    causal = jnp.arange(GROUP)[:, None] >= jnp.arange(GROUP)[None, :]
    scores = jnp.einsum('ctd,csd->cts', qc, kc)
    probs = jnp.where(causal, scores * scale, 0.0).astype(jnp.bfloat16).astype(jnp.float32)
    states = jnp.einsum('csd,cse->cde', kc, vc)
    zero_state = jnp.zeros((1, DH, DH), jnp.float32)
    before = jnp.concatenate([zero_state, jnp.cumsum(states, axis=0)[:-1]], axis=0)
    before_low = before.astype(jnp.bfloat16).astype(jnp.float32)
    attended = scale * jnp.einsum('ctd,cde->cte', qc, before_low) + jnp.einsum('cts,cse->cte', probs, vc)
    dscores = jnp.einsum('cte,cse->cts', gc, vc)
    dprobs = jnp.where(causal, dscores * scale, 0.0).astype(jnp.bfloat16).astype(jnp.float32)
    grads_state = jnp.einsum('ctd,cte->cde', qc, gc)
    later = jnp.cumsum(grads_state[::-1], axis=0)[::-1]
    after = jnp.concatenate([later[1:], zero_state], axis=0)
    after_low = after.astype(jnp.bfloat16).astype(jnp.float32)
    grad_q = scale * jnp.einsum('cte,cde->ctd', gc, before_low) + jnp.einsum('cts,csd->ctd', dprobs, kc)
    grad_k = scale * jnp.einsum('cse,cde->csd', vc, after_low) + jnp.einsum('cts,ctd->csd', dprobs, qc)
    grad_v = scale * jnp.einsum('csd,cde->cse', kc, after_low) + jnp.einsum('cts,cte->cse', probs, gc)
    shape = (blocks * GROUP, DH)
    return (attended.reshape(shape).astype(jnp.bfloat16), grad_q.reshape(shape).astype(jnp.bfloat16),
            grad_k.reshape(shape).astype(jnp.bfloat16), grad_v.reshape(shape).astype(jnp.bfloat16))


def reference(queries, keys, values, grad_out):
    def split_heads(array):
        return jnp.moveaxis(array.reshape(TOKENS, HEADS, DH), 1, 0)

    results = lax.map(one_head, (split_heads(queries), split_heads(keys), split_heads(values), split_heads(grad_out)))

    def join_heads(array):
        return jnp.moveaxis(array, 0, 1).reshape(TOKENS, HEADS * DH)

    return (join_heads(results[0]), join_heads(results[1]), join_heads(results[2]), join_heads(results[3]))
```

```python
import functools

import jax
import jax.numpy as jnp
from jax import lax
from jax.experimental import pallas as pl
from jax.experimental.pallas import tpu as pltpu
from jax.sharding import PartitionSpec as P

DH = 128
GROUP = 256
MEMBERS = 8
MESH = pl.DeviceIdType.MESH


def dot(a, b, a_dim, b_dim):
    return lax.dot_general(a, b, (((a_dim,), (b_dim,)), ((), ())), preferred_element_type=jnp.float32)


def carry_kernel(
    scale, groups, q_hbm, k_hbm, v_hbm, g_hbm,
    q, k, v, g, part, inner, carry,
    load_sem, own, got, totals, far, back, send_sem, recv_sem,
):
    rows, width = q.shape
    blocks, heads = rows // GROUP, width // DH
    piece = heads * DH // MEMBERS
    head = lax.axis_index("head")
    me = lax.axis_index("seq")
    group, member = me // MEMBERS, lax.rem(me, MEMBERS)
    mates = [lax.rem(member + i, MEMBERS) for i in range(1, MEMBERS)]
    others = [lax.rem(group + i, groups) for i in range(1, groups)]

    def at(a_group, a_member):
        return (a_group * MEMBERS + a_member, head)

    barrier = pltpu.get_barrier_semaphore()
    for j in mates:
        pl.semaphore_signal(barrier, inc=1, device_id=at(group, j), device_id_type=MESH)
    for j in others:
        pl.semaphore_signal(barrier, inc=1, device_id=at(j, member), device_id_type=MESH)

    loads = [
        pltpu.make_async_copy(src, dst, load_sem.at[i])
        for i, (src, dst) in enumerate(((k_hbm, k), (v_hbm, v), (q_hbm, q), (g_hbm, g)))
    ]
    for load in loads:
        load.start()

    def head_of(ref, block, h):
        return ref[pl.ds(pl.multiple_of(block * GROUP, GROUP), GROUP), h * DH : (h + 1) * DH]

    def states(left, right, way, order):
        sums = [jnp.zeros((DH, DH), jnp.float32) for _ in range(heads)]
        for block in order:
            for h in range(heads):
                inner[way, block, h * DH : (h + 1) * DH, :] = sums[h]
                sums[h] = sums[h] + dot(head_of(left, block, h), head_of(right, block, h), 0, 0)
        for j in range(MEMBERS):
            h, row = divmod(j * piece, DH)
            own[j, way] = sums[h][row : row + piece]

    loads[0].wait()
    loads[1].wait()
    states(k, v, 0, range(blocks))
    loads[2].wait()
    loads[3].wait()
    states(q, g, 1, reversed(range(blocks)))
    pl.semaphore_wait(barrier, MEMBERS + groups - 2)

    def send(src, dst, step, target):
        return pltpu.make_async_remote_copy(
            src_ref=src, dst_ref=dst, send_sem=send_sem.at[step], recv_sem=recv_sem.at[step],
            device_id=target, device_id_type=MESH,
        )

    def arrive(buffer, count, step):
        ref = buffer.at[pl.ds(0, count)]
        pltpu.make_async_copy(ref, ref, recv_sem.at[step]).wait()

    def sent(buffer, count, step):
        ref = buffer.at[pl.ds(0, count)]
        pltpu.make_async_copy(ref, ref, send_sem.at[step]).wait()

    causal = lax.broadcasted_iota(jnp.int32, (GROUP, GROUP), 0) >= lax.broadcasted_iota(
        jnp.int32, (GROUP, GROUP), 1
    )

    def within(block, carried):
        here = pl.ds(pl.multiple_of(block * GROUP, GROUP), GROUP)
        for h in range(heads):
            cols = slice(h * DH, (h + 1) * DH)
            qb, kb, vb, gb = (head_of(ref, block, h) for ref in (q, k, v, g))
            probs = jnp.where(causal, dot(qb, kb, 1, 1) * scale, 0.0).astype(jnp.bfloat16)
            part[0, here, cols] = dot(probs, vb, 1, 0)
            part[3, here, cols] = dot(probs, gb, 0, 0)
            dprobs = jnp.where(causal, dot(gb, vb, 1, 1) * scale, 0.0).astype(jnp.bfloat16)
            part[1, here, cols] = dot(dprobs, kb, 1, 0)
            part[2, here, cols] = dot(dprobs, qb, 0, 0)
        return carried

    for j in mates:
        send(own.at[j], got.at[member], 0, at(group, j)).start()
    got[member] = own[member]
    lax.fori_loop(0, 2, within, 0)
    arrive(got, MEMBERS - 1, 0)
    total = got[0]
    for j in range(1, MEMBERS):
        total = total + got[j]
    totals[...] = total
    for j in others:
        way = jnp.where(j > group, 0, 1)
        send(totals.at[way], far.at[group], 1, at(j, member)).start()
    far[group] = jnp.zeros(far.shape[1:], jnp.float32)
    lax.fori_loop(2, 4, within, 0)
    arrive(far, groups - 1, 1)
    before = jnp.zeros(far.shape[1:], jnp.float32)
    after = jnp.zeros(far.shape[1:], jnp.float32)
    for j in range(groups):
        before = before + jnp.where(j < group, far[j], 0.0)
        after = after + jnp.where(j > group, far[j], 0.0)
    for j in range(MEMBERS):
        back[j, 0] = before
        before = before + got[j, 0]
    for j in reversed(range(MEMBERS)):
        back[j, 1] = after
        after = after + got[j, 1]
    for j in mates:
        send(back.at[j], carry.at[member], 2, at(group, j)).start()
    carry[member] = back[member]
    lax.fori_loop(4, blocks, within, 0)
    sent(own, MEMBERS - 1, 0)
    sent(far, groups - 1, 1)
    sent(back, MEMBERS - 1, 2)
    arrive(carry, MEMBERS - 1, 2)


def final_kernel(scale, q, k, v, g, part, inner, carry, *rest):
    outs, (weight, ready, sem) = rest[:4], rest[4:]
    rows, width = q.shape
    blocks, heads = rows // GROUP, width // DH
    zeros = jnp.zeros((DH, DH), jnp.bfloat16)
    stores = []
    for block in range(blocks):
        here = pl.ds(block * GROUP, GROUP)
        for way in range(2):
            entering = carry[:, way].reshape(heads * DH, DH) + inner[way, block]
            low = entering.astype(jnp.bfloat16)
            for h in range(heads):
                for other in range(heads):
                    weight[block, way, h * DH : (h + 1) * DH, other * DH : (other + 1) * DH] = (
                        low[h * DH : (h + 1) * DH] if h == other else zeros
                    )
        for i, (ref, way, dim) in enumerate(((q, 0, 0), (g, 0, 1), (v, 1, 1), (k, 1, 0))):
            value = scale * dot(ref[here], weight[block, way], 1, dim) + part[i, here]
            ready[i, here] = value.astype(jnp.bfloat16)
            store = pltpu.make_async_copy(ready.at[i, here], outs[i].at[here], sem.at[i, block])
            store.start()
            stores.append(store)
    for store in stores:
        store.wait()


def shards(queries, keys, values, grad_out):
    rows, width = queries.shape
    blocks, heads = rows // GROUP, width // DH
    count = lax.axis_size("seq")
    groups = count // MEMBERS
    piece = heads * DH // MEMBERS
    scale = (DH * rows * count) ** (-0.5)
    any_space = pl.BlockSpec(memory_space=pl.ANY)
    vmem = pl.BlockSpec(memory_space=pltpu.VMEM)
    f32 = jnp.float32
    low = pltpu.VMEM((rows, width), jnp.bfloat16)
    operands = [pltpu.with_memory_space_constraint(x, pltpu.HBM) for x in (queries, keys, values, grad_out)]
    held = pl.pallas_call(
        functools.partial(carry_kernel, scale, groups),
        out_shape=(
            low, low, low, low,
            pltpu.VMEM((4, rows, width), f32),
            pltpu.VMEM((2, blocks, heads * DH, DH), f32),
            pltpu.VMEM((MEMBERS, 2, piece, DH), f32),
        ),
        in_specs=[any_space] * 4,
        out_specs=(vmem,) * 7,
        scratch_shapes=[
            pltpu.SemaphoreType.DMA((4,)),
            pltpu.VMEM((MEMBERS, 2, piece, DH), f32),
            pltpu.VMEM((MEMBERS, 2, piece, DH), f32),
            pltpu.VMEM((2, piece, DH), f32),
            pltpu.VMEM((groups, piece, DH), f32),
            pltpu.VMEM((MEMBERS, 2, piece, DH), f32),
            pltpu.SemaphoreType.DMA((3,)),
            pltpu.SemaphoreType.DMA((3,)),
        ],
        compiler_params=pltpu.CompilerParams(
            collective_id=0, has_side_effects=True, vmem_limit_bytes=32 * 1024 * 1024
        ),
        name="scan_and_blocks",
    )(*operands)
    held = [pltpu.with_memory_space_constraint(x, pltpu.VMEM) for x in held]
    out = jax.ShapeDtypeStruct((rows, width), jnp.bfloat16)
    return pl.pallas_call(
        functools.partial(final_kernel, scale),
        out_shape=(out,) * 4,
        in_specs=[vmem] * 7,
        out_specs=(any_space,) * 4,
        scratch_shapes=[
            pltpu.VMEM((blocks, 2, width, width), jnp.bfloat16),
            pltpu.VMEM((4, rows, width), jnp.bfloat16),
            pltpu.SemaphoreType.DMA((4, blocks)),
        ],
        compiler_params=pltpu.CompilerParams(vmem_limit_bytes=32 * 1024 * 1024),
        name="across_blocks",
    )(*held)


def solution(mesh):
    placed = (P("seq", "head"),) * 4
    return jax.shard_map(shards, mesh=mesh, in_specs=placed, out_specs=placed, check_vma=False)
```

```python
import functools

import jax
import jax.numpy as jnp
from jax import lax
from jax.experimental import pallas as pl
from jax.experimental.pallas import tpu as pltpu
from jax.sharding import PartitionSpec as P

DH = 128
GROUP = 256
MEMBERS = 8
BEFORE, AFTER = 0, 1
MESH = pl.DeviceIdType.MESH


def dot(a, b, a_dim, b_dim):
    return lax.dot_general(a, b, (((a_dim,), (b_dim,)), ((), ())), preferred_element_type=jnp.float32)


def across(scale, refs, dims, entering, inner, part, weight, ready, done=None):
    rows, width = refs[0].shape
    heads = width // DH
    zeros = jnp.zeros((DH, DH), jnp.bfloat16)
    state = entering[...].reshape(heads * DH, DH)
    for block in range(rows // GROUP):
        here = pl.ds(block * GROUP, GROUP)
        low = (state + inner[block]).astype(jnp.bfloat16)
        for h in range(heads):
            for other in range(heads):
                weight[block, h * DH : (h + 1) * DH, other * DH : (other + 1) * DH] = (
                    low[h * DH : (h + 1) * DH] if h == other else zeros
                )
        for i, (ref, dim) in enumerate(zip(refs, dims, strict=True)):
            value = scale * dot(ref[here], weight[block], 1, dim) + part[i, here]
            ready[i, here] = value.astype(jnp.bfloat16)
            if done is not None:
                done(i, block)


def carry_kernel(
    scale, groups, q_hbm, k_hbm, v_hbm, g_hbm,
    k, v, early, part, inner, carry,
    q, g, early_part, early_inner, early_carry, weight, own, got, totals, far, back,
    load_sem, send_sem, recv_sem, far_sem, higher_sem,
):
    rows, width = q.shape
    blocks, heads = rows // GROUP, width // DH
    piece = heads * DH // MEMBERS
    head = lax.axis_index("head")
    me = lax.axis_index("seq")
    group, member = me // MEMBERS, lax.rem(me, MEMBERS)
    mates = [lax.rem(member + i, MEMBERS) for i in (6, 2, 5, 1, 7, 3, 4)]
    inners, carries = (early_inner, inner), (early_carry, carry)

    def at(a_group, a_member):
        return (a_group * MEMBERS + a_member, head)

    def tell(sem, target):
        pl.semaphore_signal(sem, inc=1, device_id=target, device_id_type=MESH)

    loads = [
        pltpu.make_async_copy(src, dst, load_sem.at[i])
        for i, (src, dst) in enumerate(((q_hbm, q), (g_hbm, g), (k_hbm, k), (v_hbm, v)))
    ]
    loads[0].start()
    loads[1].start()
    far[...] = jnp.zeros_like(far)
    barrier = pltpu.get_barrier_semaphore()
    for j in mates:
        tell(barrier, at(group, j))
    for j in range(1, groups):

        @pl.when(j > group)
        def _():
            tell(barrier, at(j, member))

    def states(left, right, way, order):
        sums = [jnp.zeros((DH, DH), jnp.float32) for _ in range(heads)]
        for block in order:
            here = slice(block * GROUP, (block + 1) * GROUP)
            for h in range(heads):
                cols = slice(h * DH, (h + 1) * DH)
                inners[way][block, cols] = sums[h]
                sums[h] = sums[h] + dot(left[here, cols], right[here, cols], 0, 0)
        for j in range(MEMBERS):
            h, row = divmod(j * piece, DH)
            own[way, j] = sums[h][row : row + piece]

    def send(src, dst, send_at, recv_at, target):
        pltpu.make_async_remote_copy(
            src_ref=src, dst_ref=dst, send_sem=send_at, recv_sem=recv_at,
            device_id=target, device_id_type=MESH,
        ).start()

    def wait(ref, sem):
        pltpu.make_async_copy(ref, ref, sem).wait()

    def answer():
        for j in range(groups - 1):

            @pl.when(j < group)
            def _():
                tell(higher_sem, at(j, member))

    def scatter(way):
        for j in mates:
            send(own.at[way, j], got.at[way, member], send_sem.at[way, 0], recv_sem.at[way, 0], at(group, j))
        got[way, member] = own[way, member]

    def exchange(way):
        wait(got.at[way, pl.ds(0, MEMBERS - 1)], recv_sem.at[way, 0])
        total = got[way, 0]
        for j in range(1, MEMBERS):
            total = total + got[way, j]
        totals[way] = total
        if way == BEFORE:

            @pl.when(group < groups - 1)
            def _():
                pl.semaphore_wait(higher_sem, groups - 1 - group)

        for j in range(groups):

            @pl.when(j > group if way == BEFORE else j < group)
            def _():
                send(
                    totals.at[way], far.at[way, group], send_sem.at[0, 1], far_sem.at[way, group],
                    at(j, member),
                )

    def give_back(way):
        for j in range(groups):

            @pl.when(j < group if way == BEFORE else j > group)
            def _():
                wait(far.at[way, j], far_sem.at[way, j])

        total = jnp.zeros((piece, DH), jnp.float32)
        for j in range(groups):
            total = total + jnp.where(j < group if way == BEFORE else j > group, far[way, j], 0.0)
        for j in range(MEMBERS) if way == BEFORE else reversed(range(MEMBERS)):
            back[way, j] = total
            total = total + got[way, j]
        for j in mates:
            send(back.at[way, j], carries[way].at[member], send_sem.at[way, 2], recv_sem.at[way, 2], at(group, j))
        carries[way][member] = back[way, member]

    causal = lax.broadcasted_iota(jnp.int32, (GROUP, GROUP), 0) >= lax.broadcasted_iota(
        jnp.int32, (GROUP, GROUP), 1
    )

    def within(block, carried):
        here = pl.ds(pl.multiple_of(block * GROUP, GROUP), GROUP)
        for h in range(heads):
            cols = slice(h * DH, (h + 1) * DH)
            qb, kb, vb, gb = (ref[here, cols] for ref in (q, k, v, g))
            probs = jnp.where(causal, dot(qb, kb, 1, 1) * scale, 0.0).astype(jnp.bfloat16)
            early_part[0, here, cols] = dot(probs, vb, 1, 0)
            part[1, here, cols] = dot(probs, gb, 0, 0)
            dprobs = jnp.where(causal, dot(gb, vb, 1, 1) * scale, 0.0).astype(jnp.bfloat16)
            early_part[1, here, cols] = dot(dprobs, kb, 1, 0)
            part[0, here, cols] = dot(dprobs, qb, 0, 0)
        return carried

    loads[0].wait()
    loads[1].wait()
    loads[2].start()
    loads[3].start()
    states(q, g, AFTER, reversed(range(blocks)))
    pl.semaphore_wait(barrier, MEMBERS - 1 + group)
    scatter(AFTER)
    answer()
    loads[2].wait()
    loads[3].wait()
    states(k, v, BEFORE, range(blocks))
    scatter(BEFORE)
    exchange(AFTER)
    lax.fori_loop(0, blocks, within, 0)
    exchange(BEFORE)
    give_back(BEFORE)
    give_back(AFTER)
    wait(early_carry.at[pl.ds(0, MEMBERS - 1)], recv_sem.at[BEFORE, 2])
    across(scale, (q, g), (0, 1), early_carry, early_inner, early_part, weight, early)
    wait(far.at[0, pl.ds(0, groups - 1)], send_sem.at[0, 1])
    for way in (BEFORE, AFTER):
        wait(own.at[way, pl.ds(0, MEMBERS - 1)], send_sem.at[way, 0])
        wait(back.at[way, pl.ds(0, MEMBERS - 1)], send_sem.at[way, 2])
    wait(carry.at[pl.ds(0, MEMBERS - 1)], recv_sem.at[AFTER, 2])


def final_kernel(scale, k, v, early, part, inner, carry, *rest):
    outs, (weight, ready, early_sem, sem) = rest[:4], rest[4:]
    stores = [pltpu.make_async_copy(early.at[i], outs[i], early_sem.at[i]) for i in range(2)]
    for store in stores:
        store.start()

    def done(i, block):
        here = pl.ds(block * GROUP, GROUP)
        store = pltpu.make_async_copy(ready.at[i, here], outs[2 + i].at[here], sem.at[i, block])
        store.start()
        stores.append(store)

    across(scale, (v, k), (1, 0), carry, inner, part, weight, ready, done)
    for store in stores:
        store.wait()


def shards(queries, keys, values, grad_out):
    rows, width = queries.shape
    blocks, heads = rows // GROUP, width // DH
    count = lax.axis_size("seq")
    groups = count // MEMBERS
    piece = heads * DH // MEMBERS
    scale = (DH * rows * count) ** (-0.5)
    anywhere = pl.BlockSpec(memory_space=pl.ANY)
    vmem = pl.BlockSpec(memory_space=pltpu.VMEM)
    f32 = jnp.float32
    array = pltpu.VMEM((rows, width), jnp.bfloat16)
    pair = pltpu.VMEM((2, rows, width), jnp.bfloat16)
    parts = pltpu.VMEM((2, rows, width), f32)
    inner = pltpu.VMEM((blocks, heads * DH, DH), f32)
    carry = pltpu.VMEM((MEMBERS, piece, DH), f32)
    weight = pltpu.VMEM((blocks, width, width), jnp.bfloat16)
    pieces = pltpu.VMEM((2, MEMBERS, piece, DH), f32)
    dma = pltpu.SemaphoreType.DMA
    operands = [
        pltpu.with_memory_space_constraint(x, pltpu.HBM) for x in (queries, keys, values, grad_out)
    ]
    held = pl.pallas_call(
        functools.partial(carry_kernel, scale, groups),
        out_shape=(array, array, pair, parts, inner, carry),
        in_specs=[anywhere] * 4,
        out_specs=(vmem,) * 6,
        scratch_shapes=[
            array, array, parts, inner, carry, weight,
            pieces, pieces, pltpu.VMEM((2, piece, DH), f32), pltpu.VMEM((2, groups, piece, DH), f32), pieces,
            dma((4,)), dma((2, 3)), dma((2, 3)), dma((2, groups)),
            pltpu.SemaphoreType.REGULAR,
        ],
        compiler_params=pltpu.CompilerParams(
            collective_id=0, has_side_effects=True, vmem_limit_bytes=32 * 1024 * 1024
        ),
        name="scan_and_blocks",
    )(*operands)
    held = [pltpu.with_memory_space_constraint(x, pltpu.VMEM) for x in held]
    out = jax.ShapeDtypeStruct((rows, width), jnp.bfloat16)
    return pl.pallas_call(
        functools.partial(final_kernel, scale),
        out_shape=(out,) * 4,
        in_specs=[vmem] * 6,
        out_specs=(anywhere,) * 4,
        scratch_shapes=[weight, pair, dma((2,)), dma((2, blocks))],
        compiler_params=pltpu.CompilerParams(vmem_limit_bytes=32 * 1024 * 1024),
        name="across_blocks",
    )(*held)


def solution(mesh):
    placed = (P("seq", "head"),) * 4
    return jax.shard_map(shards, mesh=mesh, in_specs=placed, out_specs=placed, check_vma=False)
```

```python
import functools

import jax
import jax.numpy as jnp
from jax import lax
from jax.experimental import pallas as pl
from jax.experimental.pallas import tpu as pltpu
from jax.sharding import PartitionSpec as P

DH = 128
GROUP = 256
MEMBERS = 8
BEFORE, AFTER = 0, 1
MESH = pl.DeviceIdType.MESH


def dot(a, b, a_dim, b_dim):
    return lax.dot_general(a, b, (((a_dim,), (b_dim,)), ((), ())), preferred_element_type=jnp.float32)


def across(scale, refs, dims, entering, inner, part, ready, done=None):
    rows, width = refs[0].shape
    state = entering[...].reshape(width, DH)
    for block in range(rows // GROUP):
        here = pl.ds(block * GROUP, GROUP)
        low = (state + inner[block]).astype(jnp.bfloat16)
        for i, (ref, dim) in enumerate(zip(refs, dims, strict=True)):
            for h in range(width // DH):
                cols = slice(h * DH, (h + 1) * DH)
                value = scale * dot(ref[here, cols], low[cols], 1, dim) + part[i, here, cols]
                ready[i, here, cols] = value.astype(jnp.bfloat16)
            if done is not None:
                done(i, block)


def carry_kernel(
    scale, groups, q_hbm, k_hbm, v_hbm, g_hbm,
    k, v, early, part, inner, carry,
    q, g, early_part, early_inner, early_carry, sums, own, got, totals, half_sum, far, back,
    load_sem, send_sem, recv_sem, far_send_sem, far_sem, higher_sem,
):
    rows, width = q.shape
    blocks, heads = rows // GROUP, width // DH
    piece = heads * DH // MEMBERS
    head = lax.axis_index("head")
    me = lax.axis_index("seq")
    group, member = me // MEMBERS, lax.rem(me, MEMBERS)
    mates = [lax.rem(member + i, MEMBERS) for i in (6, 2, 5, 1, 7, 3, 4)]
    half, near = groups // 2, groups // 2 - 1
    turn = MEMBERS // 2

    def turned(a_group, index):
        return lax.rem(index + jnp.where(a_group == half, turn, 0), MEMBERS)

    mine = turned(group, member)
    inners, carries = (early_inner, inner), (early_carry, carry)

    def at(a_group, a_member):
        return (a_group * MEMBERS + a_member, head)

    def tell(sem, target):
        pl.semaphore_signal(sem, inc=1, device_id=target, device_id_type=MESH)

    barrier = pltpu.get_barrier_semaphore()
    for j in mates:
        tell(barrier, at(group, j))
    for j in range(groups):

        @pl.when((j > group) & ((group < near) | (group >= half) | (j <= half)))
        def _():
            tell(barrier, at(j, turned(j, mine)))

    loads = [
        pltpu.make_async_copy(src, dst, load_sem.at[i])
        for i, (src, dst) in enumerate(((q_hbm, q), (g_hbm, g), (k_hbm, k), (v_hbm, v)))
    ]
    loads[0].start()
    loads[1].start()
    sums[...] = jnp.zeros_like(sums)

    def states(left, right, way, order):
        sums = [jnp.zeros((DH, DH), jnp.float32) for _ in range(heads)]
        for block in order:
            here = slice(block * GROUP, (block + 1) * GROUP)
            for h in range(heads):
                cols = slice(h * DH, (h + 1) * DH)
                inners[way][block, cols] = sums[h]
                sums[h] = sums[h] + dot(left[here, cols], right[here, cols], 0, 0)
        for j in range(MEMBERS):
            h, row = divmod(j * piece, DH)
            own[way, j] = sums[h][row : row + piece]

    def send(src, dst, send_at, recv_at, target):
        pltpu.make_async_remote_copy(
            src_ref=src, dst_ref=dst, send_sem=send_at, recv_sem=recv_at,
            device_id=target, device_id_type=MESH,
        ).start()

    def wait(ref, sem):
        pltpu.make_async_copy(ref, ref, sem).wait()

    def answer():
        for j in range(groups):

            @pl.when((j < group) & ((group < half) | (j >= half)))
            def _():
                tell(higher_sem, at(j, turned(j, mine)))

    def scatter(way):
        for j in mates:
            send(
                own.at[way, turned(group, j)], got.at[way, member], send_sem.at[way, 0], recv_sem.at[way, 0], at(group, j)
            )
        got[way, member] = own[way, mine]

    def collect(way):
        wait(got.at[way, pl.ds(0, MEMBERS - 1)], recv_sem.at[way, 0])
        total = got[way, 0]
        for j in range(1, MEMBERS):
            total = total + got[way, j]
        totals[way] = total

    def send_far(src, way, j):
        send(src, far.at[way, group], far_send_sem.at[way, j], far_sem.at[way, group], at(j, turned(j, mine)))

    def direct(way, j):
        if way == BEFORE:
            return (j > group) & ((group >= half) | (j < half))
        return (j < group) & ((group < half) | (j < near) | (j >= half))

    def summed(way, j):
        if way == BEFORE:
            return (group == half - 1) & (j >= half)
        return (group == half) & (near <= j < half)

    def exchange(way):
        for j in range(groups):

            @pl.when(direct(way, j))
            def _():
                send_far(totals.at[way], way, j)

    def gather(way):
        for j in range(groups) if way == BEFORE else reversed(range(groups)):
            here = (j < group) & ((group < half) | (j >= half - 1))
            if way == AFTER:
                here = (j > group) & ((group < near) | (group >= half) | (j <= half))

            @pl.when(here)
            def _():
                wait(far.at[way, j], far_sem.at[way, j])
                sums[way] += far[way, j]

    def exchange_sum(way):
        @pl.when(group == (half - 1 if way == BEFORE else half))
        def _():
            half_sum[way] = sums[way] + totals[way]
            for j in range(groups):

                @pl.when(summed(way, j))
                def _():
                    send_far(half_sum.at[way], way, j)

    def give_back(way):
        total = sums[way]
        for j in range(MEMBERS) if way == BEFORE else reversed(range(MEMBERS)):
            back[way, j] = total
            total = total + got[way, j]
        for j in mates:
            send(back.at[way, j], carries[way].at[mine], send_sem.at[way, 1], recv_sem.at[way, 1], at(group, j))
        carries[way][mine] = back[way, member]

    causal = lax.broadcasted_iota(jnp.int32, (GROUP, GROUP), 0) >= lax.broadcasted_iota(
        jnp.int32, (GROUP, GROUP), 1
    )

    def within(block, carried):
        here = pl.ds(pl.multiple_of(block * GROUP, GROUP), GROUP)
        for h in range(heads):
            cols = slice(h * DH, (h + 1) * DH)
            qb, kb, vb, gb = (ref[here, cols] for ref in (q, k, v, g))
            probs = jnp.where(causal, dot(qb, kb, 1, 1) * scale, 0.0).astype(jnp.bfloat16)
            early_part[0, here, cols] = dot(probs, vb, 1, 0)
            part[1, here, cols] = dot(probs, gb, 0, 0)
            dprobs = jnp.where(causal, dot(gb, vb, 1, 1) * scale, 0.0).astype(jnp.bfloat16)
            early_part[1, here, cols] = dot(dprobs, kb, 1, 0)
            part[0, here, cols] = dot(dprobs, qb, 0, 0)
        return carried

    loads[0].wait()
    loads[1].wait()
    loads[2].start()
    loads[3].start()
    states(q, g, AFTER, reversed(range(blocks)))
    pl.semaphore_wait(barrier, MEMBERS - 1 + jnp.where(group <= half, group, near + group - half))
    scatter(AFTER)
    answer()
    loads[2].wait()
    loads[3].wait()
    states(k, v, BEFORE, range(blocks))
    scatter(BEFORE)
    collect(AFTER)
    exchange(AFTER)

    @pl.when(group == half)
    def _():
        pl.semaphore_wait(higher_sem, groups - 1 - half)
        tell(higher_sem, at(half - 1, turned(half - 1, mine)))

    lax.fori_loop(0, 3, within, 0)
    collect(BEFORE)
    higher = jnp.where(group < half - 1, half - 1 - group, jnp.where(group == half - 1, 1, groups - 1 - group))

    @pl.when((group != half) & (group < groups - 1))
    def _():
        pl.semaphore_wait(higher_sem, higher)

    exchange(BEFORE)

    @pl.when(group < half)
    def _():
        gather(BEFORE)
        exchange_sum(BEFORE)
        give_back(BEFORE)

    lax.fori_loop(3, blocks, within, 0)

    @pl.when(group >= half)
    def _():
        gather(AFTER)
        exchange_sum(AFTER)
        give_back(AFTER)

    @pl.when(group >= half)
    def _():
        gather(BEFORE)
        give_back(BEFORE)

    @pl.when(group < half)
    def _():
        gather(AFTER)
        give_back(AFTER)

    wait(early_carry.at[pl.ds(0, MEMBERS - 1)], recv_sem.at[BEFORE, 1])
    across(scale, (q, g), (0, 1), early_carry, early_inner, early_part, early)
    for way in (BEFORE, AFTER):
        for j in range(groups):

            @pl.when(direct(way, j) | summed(way, j))
            def _():
                wait(totals.at[way], far_send_sem.at[way, j])

        wait(own.at[way, pl.ds(0, MEMBERS - 1)], send_sem.at[way, 0])
        wait(back.at[way, pl.ds(0, MEMBERS - 1)], send_sem.at[way, 1])
    wait(carry.at[pl.ds(0, MEMBERS - 1)], recv_sem.at[AFTER, 1])


def final_kernel(scale, k, v, early, part, inner, carry, *rest):
    outs, (ready, early_sem, sem) = rest[:4], rest[4:]
    stores = [pltpu.make_async_copy(early.at[i], outs[i], early_sem.at[i]) for i in range(2)]
    for store in stores:
        store.start()

    def done(i, block):
        here = pl.ds(block * GROUP, GROUP)
        store = pltpu.make_async_copy(ready.at[i, here], outs[2 + i].at[here], sem.at[i, block])
        store.start()
        stores.append(store)

    across(scale, (v, k), (1, 0), carry, inner, part, ready, done)
    for store in stores:
        store.wait()


def shards(queries, keys, values, grad_out):
    rows, width = queries.shape
    blocks, heads = rows // GROUP, width // DH
    count = lax.axis_size("seq")
    groups = count // MEMBERS
    piece = heads * DH // MEMBERS
    scale = (DH * rows * count) ** (-0.5)
    anywhere = pl.BlockSpec(memory_space=pl.ANY)
    vmem = pl.BlockSpec(memory_space=pltpu.VMEM)
    f32 = jnp.float32
    array = pltpu.VMEM((rows, width), jnp.bfloat16)
    pair = pltpu.VMEM((2, rows, width), jnp.bfloat16)
    parts = pltpu.VMEM((2, rows, width), f32)
    inner = pltpu.VMEM((blocks, heads * DH, DH), f32)
    carry = pltpu.VMEM((MEMBERS, piece, DH), f32)
    pieces = pltpu.VMEM((2, MEMBERS, piece, DH), f32)
    dma = pltpu.SemaphoreType.DMA
    operands = [
        pltpu.with_memory_space_constraint(x, pltpu.HBM) for x in (queries, keys, values, grad_out)
    ]
    held = pl.pallas_call(
        functools.partial(carry_kernel, scale, groups),
        out_shape=(array, array, pair, parts, inner, carry),
        in_specs=[anywhere] * 4,
        out_specs=(vmem,) * 6,
        scratch_shapes=[
            array, array, parts, inner, carry, pltpu.VMEM((2, piece, DH), f32),
            pieces, pieces, pltpu.VMEM((2, piece, DH), f32), pltpu.VMEM((2, piece, DH), f32),
            pltpu.VMEM((2, groups, piece, DH), f32), pieces,
            dma((4,)), dma((2, 2)), dma((2, 2)), dma((2, groups)), dma((2, groups)),
            pltpu.SemaphoreType.REGULAR,
        ],
        compiler_params=pltpu.CompilerParams(
            collective_id=0, has_side_effects=True, vmem_limit_bytes=32 * 1024 * 1024
        ),
        name="scan_and_blocks",
    )(*operands)
    held = [pltpu.with_memory_space_constraint(x, pltpu.VMEM) for x in held]
    out = jax.ShapeDtypeStruct((rows, width), jnp.bfloat16)
    return pl.pallas_call(
        functools.partial(final_kernel, scale),
        out_shape=(out,) * 4,
        in_specs=[vmem] * 6,
        out_specs=(anywhere,) * 4,
        scratch_shapes=[pair, dma((2,)), dma((2, blocks))],
        compiler_params=pltpu.CompilerParams(vmem_limit_bytes=32 * 1024 * 1024),
        name="across_blocks",
    )(*held)


def solution(mesh):
    placed = (P("seq", "head"),) * 4
    return jax.shard_map(shards, mesh=mesh, in_specs=placed, out_specs=placed, check_vma=False)
```

```python
import functools

import jax
import jax.numpy as jnp
from jax import lax
from jax.experimental import pallas as pl
from jax.experimental.pallas import tpu as pltpu
from jax.sharding import PartitionSpec as P

DH = 128
GROUP = 256
MEMBERS = 8
BEFORE, AFTER = 0, 1
MESH = pl.DeviceIdType.MESH


def dot(a, b, a_dim, b_dim):
    return lax.dot_general(a, b, (((a_dim,), (b_dim,)), ((), ())), preferred_element_type=jnp.float32)


def across(scale, refs, dims, entering, inner, part, ready, done=None):
    rows, width = refs[0].shape
    state = entering[...].reshape(width, DH)
    for block in range(rows // GROUP):
        here = pl.ds(block * GROUP, GROUP)
        low = (state + inner[block]).astype(jnp.bfloat16)
        for i, (ref, dim) in enumerate(zip(refs, dims, strict=True)):
            for h in range(width // DH):
                cols = slice(h * DH, (h + 1) * DH)
                value = scale * dot(ref[here, cols], low[cols], 1, dim) + part[i, here, cols]
                ready[i, here, cols] = value.astype(jnp.bfloat16)
            if done is not None:
                done(i, block)


def carry_kernel(
    scale, groups, q_hbm, k_hbm, v_hbm, g_hbm,
    k, v, early, part, inner, carry,
    q, g, early_part, early_inner, early_carry, sums, own, got, totals, half_sum, far, back,
    load_sem, send_sem, recv_sem, far_send_sem, far_sem, higher_sem,
):
    rows, width = q.shape
    blocks, heads = rows // GROUP, width // DH
    piece = heads * DH // MEMBERS
    head = lax.axis_index("head")
    me = lax.axis_index("seq")
    group, member = me // MEMBERS, lax.rem(me, MEMBERS)
    mates = [lax.rem(member + i, MEMBERS) for i in (6, 2, 5, 1, 7, 3, 4)]
    half, near = groups // 2, groups // 2 - 1
    turn = MEMBERS // 2

    def turned(a_group, index):
        return lax.rem(index + jnp.where(a_group == half, turn, 0), MEMBERS)

    mine = turned(group, member)
    inners, carries = (early_inner, inner), (early_carry, carry)

    def at(a_group, a_member):
        return (a_group * MEMBERS + a_member, head)

    def tell(sem, target):
        pl.semaphore_signal(sem, inc=1, device_id=target, device_id_type=MESH)

    barrier = pltpu.get_barrier_semaphore()
    for j in mates:
        tell(barrier, at(group, j))
    for j in range(groups):

        @pl.when((j > group) & ((group < near) | (group >= half) | (j <= half)))
        def _():
            tell(barrier, at(j, turned(j, mine)))

    loads = [
        pltpu.make_async_copy(src, dst, load_sem.at[i])
        for i, (src, dst) in enumerate(((q_hbm, q), (g_hbm, g), (k_hbm, k), (v_hbm, v)))
    ]
    loads[0].start()
    loads[1].start()
    sums[...] = jnp.zeros_like(sums)

    def states(left, right, way, order):
        sums = [jnp.zeros((DH, DH), jnp.float32) for _ in range(heads)]
        for block in order:
            here = slice(block * GROUP, (block + 1) * GROUP)
            for h in range(heads):
                cols = slice(h * DH, (h + 1) * DH)
                inners[way][block, cols] = sums[h]
                sums[h] = sums[h] + dot(left[here, cols], right[here, cols], 0, 0)
        for j in range(MEMBERS):
            h, row = divmod(j * piece, DH)
            own[way, j] = sums[h][row : row + piece]

    def send(src, dst, send_at, recv_at, target):
        pltpu.make_async_remote_copy(
            src_ref=src, dst_ref=dst, send_sem=send_at, recv_sem=recv_at,
            device_id=target, device_id_type=MESH,
        ).start()

    def wait(ref, sem):
        pltpu.make_async_copy(ref, ref, sem).wait()

    def answer():
        for j in range(groups):

            @pl.when((j < group) & ((group < half) | (j >= half)))
            def _():
                tell(higher_sem, at(j, turned(j, mine)))

    def scatter(way):
        for j in mates:
            send(
                own.at[way, turned(group, j)], got.at[way, member], send_sem.at[way, 0], recv_sem.at[way, 0], at(group, j)
            )
        got[way, member] = own[way, mine]

    def collect(way):
        wait(got.at[way, pl.ds(0, MEMBERS - 1)], recv_sem.at[way, 0])
        total = got[way, 0]
        for j in range(1, MEMBERS):
            total = total + got[way, j]
        totals[way] = total

    def send_far(src, way, j):
        send(src, far.at[way, group], far_send_sem.at[way, j], far_sem.at[way, group], at(j, turned(j, mine)))

    def direct(way, j):
        if way == BEFORE:
            return (j > group) & ((group >= half) | (j < half))
        return (j < group) & ((group < half) | (j < near) | (j >= half))

    def summed(way, j):
        if way == BEFORE:
            return (group == half - 1) & (j >= half)
        return (group == half) & (near <= j < half)

    def exchange(way):
        for j in range(groups):

            @pl.when(direct(way, j))
            def _():
                send_far(totals.at[way], way, j)

    def gather(way):
        for j in range(groups) if way == BEFORE else reversed(range(groups)):
            here = (j < group) & ((group < half) | (j >= half - 1))
            if way == AFTER:
                here = (j > group) & ((group < near) | (group >= half) | (j <= half))

            @pl.when(here)
            def _():
                wait(far.at[way, j], far_sem.at[way, j])
                sums[way] += far[way, j]

    def exchange_sum(way):
        @pl.when(group == (half - 1 if way == BEFORE else half))
        def _():
            half_sum[way] = sums[way] + totals[way]
            for j in range(groups):

                @pl.when(summed(way, j))
                def _():
                    send_far(half_sum.at[way], way, j)

    def give_back(way):
        total = sums[way]
        for j in range(MEMBERS) if way == BEFORE else reversed(range(MEMBERS)):
            back[way, j] = total
            total = total + got[way, j]
        for j in mates:
            send(back.at[way, j], carries[way].at[mine], send_sem.at[way, 1], recv_sem.at[way, 1], at(group, j))
        carries[way][mine] = back[way, member]

    causal = lax.broadcasted_iota(jnp.int32, (GROUP, GROUP), 0) >= lax.broadcasted_iota(
        jnp.int32, (GROUP, GROUP), 1
    )

    def within(block, carried):
        here = pl.ds(pl.multiple_of(block * GROUP, GROUP), GROUP)
        for h in range(heads):
            cols = slice(h * DH, (h + 1) * DH)
            qb, kb, vb, gb = (ref[here, cols] for ref in (q, k, v, g))
            probs = jnp.where(causal, dot(qb, kb, 1, 1) * scale, 0.0).astype(jnp.bfloat16)
            early_part[0, here, cols] = dot(probs, vb, 1, 0)
            part[1, here, cols] = dot(probs, gb, 0, 0)
            dprobs = jnp.where(causal, dot(gb, vb, 1, 1) * scale, 0.0).astype(jnp.bfloat16)
            early_part[1, here, cols] = dot(dprobs, kb, 1, 0)
            part[0, here, cols] = dot(dprobs, qb, 0, 0)
        return carried

    loads[0].wait()
    loads[1].wait()
    loads[2].start()
    loads[3].start()
    states(q, g, AFTER, reversed(range(blocks)))
    pl.semaphore_wait(barrier, MEMBERS - 1 + jnp.where(group <= half, group, near + group - half))
    scatter(AFTER)
    answer()
    loads[2].wait()
    loads[3].wait()
    states(k, v, BEFORE, range(blocks))
    scatter(BEFORE)
    collect(AFTER)
    exchange(AFTER)

    @pl.when(group == half)
    def _():
        pl.semaphore_wait(higher_sem, groups - 1 - half)
        tell(higher_sem, at(half - 1, turned(half - 1, mine)))

    lax.fori_loop(0, 2, within, 0)
    collect(BEFORE)
    higher = jnp.where(group < half - 1, half - 1 - group, jnp.where(group == half - 1, 1, groups - 1 - group))

    @pl.when((group != half) & (group < groups - 1))
    def _():
        pl.semaphore_wait(higher_sem, higher)

    exchange(BEFORE)

    @pl.when(group < half)
    def _():
        gather(BEFORE)
        exchange_sum(BEFORE)
        give_back(BEFORE)

    lax.fori_loop(2, blocks, within, 0)

    @pl.when(group >= half)
    def _():
        gather(AFTER)
        exchange_sum(AFTER)
        give_back(AFTER)

    @pl.when(group >= half)
    def _():
        gather(BEFORE)
        give_back(BEFORE)

    @pl.when(group < half)
    def _():
        gather(AFTER)
        give_back(AFTER)

    wait(early_carry.at[pl.ds(0, MEMBERS - 1)], recv_sem.at[BEFORE, 1])
    across(scale, (q, g), (0, 1), early_carry, early_inner, early_part, early)
    for way in (BEFORE, AFTER):
        for j in range(groups):

            @pl.when(direct(way, j) | summed(way, j))
            def _():
                wait(totals.at[way], far_send_sem.at[way, j])

        wait(own.at[way, pl.ds(0, MEMBERS - 1)], send_sem.at[way, 0])
        wait(back.at[way, pl.ds(0, MEMBERS - 1)], send_sem.at[way, 1])
    wait(carry.at[pl.ds(0, MEMBERS - 1)], recv_sem.at[AFTER, 1])


def final_kernel(scale, k, v, early, part, inner, carry, *rest):
    outs, (ready, early_sem, sem) = rest[:4], rest[4:]
    stores = [pltpu.make_async_copy(early.at[i], outs[i], early_sem.at[i]) for i in range(2)]
    for store in stores:
        store.start()

    def done(i, block):
        here = pl.ds(block * GROUP, GROUP)
        store = pltpu.make_async_copy(ready.at[i, here], outs[2 + i].at[here], sem.at[i, block])
        store.start()
        stores.append(store)

    across(scale, (v, k), (1, 0), carry, inner, part, ready, done)
    for store in stores:
        store.wait()


def shards(queries, keys, values, grad_out):
    rows, width = queries.shape
    blocks, heads = rows // GROUP, width // DH
    count = lax.axis_size("seq")
    groups = count // MEMBERS
    piece = heads * DH // MEMBERS
    scale = (DH * rows * count) ** (-0.5)
    anywhere = pl.BlockSpec(memory_space=pl.ANY)
    vmem = pl.BlockSpec(memory_space=pltpu.VMEM)
    f32 = jnp.float32
    array = pltpu.VMEM((rows, width), jnp.bfloat16)
    pair = pltpu.VMEM((2, rows, width), jnp.bfloat16)
    parts = pltpu.VMEM((2, rows, width), f32)
    inner = pltpu.VMEM((blocks, heads * DH, DH), f32)
    carry = pltpu.VMEM((MEMBERS, piece, DH), f32)
    pieces = pltpu.VMEM((2, MEMBERS, piece, DH), f32)
    dma = pltpu.SemaphoreType.DMA
    operands = [
        pltpu.with_memory_space_constraint(x, pltpu.HBM) for x in (queries, keys, values, grad_out)
    ]
    held = pl.pallas_call(
        functools.partial(carry_kernel, scale, groups),
        out_shape=(array, array, pair, parts, inner, carry),
        in_specs=[anywhere] * 4,
        out_specs=(vmem,) * 6,
        scratch_shapes=[
            array, array, parts, inner, carry, pltpu.VMEM((2, piece, DH), f32),
            pieces, pieces, pltpu.VMEM((2, piece, DH), f32), pltpu.VMEM((2, piece, DH), f32),
            pltpu.VMEM((2, groups, piece, DH), f32), pieces,
            dma((4,)), dma((2, 2)), dma((2, 2)), dma((2, groups)), dma((2, groups)),
            pltpu.SemaphoreType.REGULAR,
        ],
        compiler_params=pltpu.CompilerParams(
            collective_id=0, has_side_effects=True, vmem_limit_bytes=32 * 1024 * 1024
        ),
        name="scan_and_blocks",
    )(*operands)
    held = [pltpu.with_memory_space_constraint(x, pltpu.VMEM) for x in held]
    out = jax.ShapeDtypeStruct((rows, width), jnp.bfloat16)
    return pl.pallas_call(
        functools.partial(final_kernel, scale),
        out_shape=(out,) * 4,
        in_specs=[vmem] * 6,
        out_specs=(anywhere,) * 4,
        scratch_shapes=[pair, dma((2,)), dma((2, blocks))],
        compiler_params=pltpu.CompilerParams(vmem_limit_bytes=32 * 1024 * 1024),
        name="across_blocks",
    )(*held)


def solution(mesh):
    placed = (P("seq", "head"),) * 4
    return jax.shard_map(shards, mesh=mesh, in_specs=placed, out_specs=placed, check_vma=False)
```

```python
import functools

import jax
import jax.numpy as jnp
from jax import lax
from jax.experimental import pallas as pl
from jax.experimental.pallas import tpu as pltpu
from jax.sharding import PartitionSpec as P

DH = 128
GROUP = 256
MEMBERS = 8
BEFORE, AFTER = 0, 1
MESH = pl.DeviceIdType.MESH


def dot(a, b, a_dim, b_dim):
    return lax.dot_general(a, b, (((a_dim,), (b_dim,)), ((), ())), preferred_element_type=jnp.float32)


def across(scale, refs, dims, entering, inner, part, ready, done=None):
    rows, width = refs[0].shape
    state = entering[...].reshape(width, DH)
    for block in range(rows // GROUP):
        here = pl.ds(block * GROUP, GROUP)
        low = (state + inner[block]).astype(jnp.bfloat16)
        for i, (ref, dim) in enumerate(zip(refs, dims, strict=True)):
            for h in range(width // DH):
                cols = slice(h * DH, (h + 1) * DH)
                value = scale * dot(ref[here, cols], low[cols], 1, dim) + part[i, here, cols]
                ready[i, here, cols] = value.astype(jnp.bfloat16)
            if done is not None:
                done(i, block)


def carry_kernel(
    scale, groups, q_hbm, k_hbm, v_hbm, g_hbm,
    k, v, early, part, inner, carry,
    q, g, early_part, early_inner, early_carry, sums, own, got, totals, half_sum, far, back,
    load_sem, send_sem, recv_sem, far_send_sem, far_sem, higher_sem,
):
    rows, width = q.shape
    blocks, heads = rows // GROUP, width // DH
    piece = heads * DH // MEMBERS
    head = lax.axis_index("head")
    me = lax.axis_index("seq")
    group, member = me // MEMBERS, lax.rem(me, MEMBERS)
    mates = [lax.rem(member + i, MEMBERS) for i in (6, 2, 5, 1, 7, 3, 4)]
    half, near = groups // 2, groups // 2 - 1
    turn = MEMBERS // 2

    def turned(a_group, index):
        return lax.rem(index + jnp.where(a_group == half, turn, 0), MEMBERS)

    mine = turned(group, member)
    inners, carries = (early_inner, inner), (early_carry, carry)

    def at(a_group, a_member):
        return (a_group * MEMBERS + a_member, head)

    def tell(sem, target):
        pl.semaphore_signal(sem, inc=1, device_id=target, device_id_type=MESH)

    barrier = pltpu.get_barrier_semaphore()
    for j in mates:
        tell(barrier, at(group, j))
    for j in range(groups):

        @pl.when((j > group) & ((group < near) | (group >= half) | (j <= half)))
        def _():
            tell(barrier, at(j, turned(j, mine)))

    loads = [
        pltpu.make_async_copy(src, dst, load_sem.at[i])
        for i, (src, dst) in enumerate(((q_hbm, q), (g_hbm, g), (k_hbm, k), (v_hbm, v)))
    ]
    loads[0].start()
    loads[1].start()
    sums[...] = jnp.zeros_like(sums)

    def states(left, right, way, order):
        sums = [jnp.zeros((DH, DH), jnp.float32) for _ in range(heads)]
        for block in order:
            here = slice(block * GROUP, (block + 1) * GROUP)
            for h in range(heads):
                cols = slice(h * DH, (h + 1) * DH)
                inners[way][block, cols] = sums[h]
                sums[h] = sums[h] + dot(left[here, cols], right[here, cols], 0, 0)
        for j in range(MEMBERS):
            h, row = divmod(j * piece, DH)
            own[way, j] = sums[h][row : row + piece]

    def send(src, dst, send_at, recv_at, target):
        pltpu.make_async_remote_copy(
            src_ref=src, dst_ref=dst, send_sem=send_at, recv_sem=recv_at,
            device_id=target, device_id_type=MESH,
        ).start()

    def wait(ref, sem):
        pltpu.make_async_copy(ref, ref, sem).wait()

    def answer():
        for j in range(groups):

            @pl.when((j < group) & ((group < half) | (j >= half)))
            def _():
                tell(higher_sem, at(j, turned(j, mine)))

    def scatter(way):
        for j in mates:
            send(
                own.at[way, turned(group, j)], got.at[way, member], send_sem.at[way, 0], recv_sem.at[way, 0], at(group, j)
            )
        got[way, member] = own[way, mine]

    def collect(way):
        wait(got.at[way, pl.ds(0, MEMBERS - 1)], recv_sem.at[way, 0])
        total = got[way, 0]
        for j in range(1, MEMBERS):
            total = total + got[way, j]
        totals[way] = total

    def send_far(src, way, j):
        send(src, far.at[way, group], far_send_sem.at[way, j], far_sem.at[way, group], at(j, turned(j, mine)))

    def direct(way, j):
        if way == BEFORE:
            return (j > group) & ((group >= half) | (j < half))
        return (j < group) & ((group < half) | (j < near) | (j >= half))

    def summed(way, j):
        if way == BEFORE:
            return (group == half - 1) & (j >= half)
        return (group == half) & (near <= j < half)

    def exchange(way, those):
        for j in those:

            @pl.when(direct(way, j))
            def _():
                send_far(totals.at[way], way, j)

    def gather(way):
        for j in range(groups) if way == BEFORE else reversed(range(groups)):
            here = (j < group) & ((group < half) | (j >= half - 1))
            if way == AFTER:
                here = (j > group) & ((group < near) | (group >= half) | (j <= half))

            @pl.when(here)
            def _():
                wait(far.at[way, j], far_sem.at[way, j])
                sums[way] += far[way, j]

    def exchange_sum(way):
        @pl.when(group == (half - 1 if way == BEFORE else half))
        def _():
            half_sum[way] = sums[way] + totals[way]
            for j in range(groups):

                @pl.when(summed(way, j))
                def _():
                    send_far(half_sum.at[way], way, j)

    def give_back(way):
        total = sums[way]
        for j in range(MEMBERS) if way == BEFORE else reversed(range(MEMBERS)):
            back[way, j] = total
            total = total + got[way, j]
        for j in mates:
            send(back.at[way, j], carries[way].at[mine], send_sem.at[way, 1], recv_sem.at[way, 1], at(group, j))
        carries[way][mine] = back[way, member]

    causal = lax.broadcasted_iota(jnp.int32, (GROUP, GROUP), 0) >= lax.broadcasted_iota(
        jnp.int32, (GROUP, GROUP), 1
    )

    def within(block, carried):
        here = pl.ds(pl.multiple_of(block * GROUP, GROUP), GROUP)
        for h in range(heads):
            cols = slice(h * DH, (h + 1) * DH)
            qb, kb, vb, gb = (ref[here, cols] for ref in (q, k, v, g))
            probs = jnp.where(causal, dot(qb, kb, 1, 1) * scale, 0.0).astype(jnp.bfloat16)
            early_part[0, here, cols] = dot(probs, vb, 1, 0)
            part[1, here, cols] = dot(probs, gb, 0, 0)
            dprobs = jnp.where(causal, dot(gb, vb, 1, 1) * scale, 0.0).astype(jnp.bfloat16)
            early_part[1, here, cols] = dot(dprobs, kb, 1, 0)
            part[0, here, cols] = dot(dprobs, qb, 0, 0)
        return carried

    loads[0].wait()
    loads[1].wait()
    loads[2].start()
    loads[3].start()
    states(q, g, AFTER, reversed(range(blocks)))
    pl.semaphore_wait(barrier, MEMBERS - 1 + jnp.where(group <= half, group, near + group - half))
    scatter(AFTER)
    answer()
    loads[2].wait()
    loads[3].wait()
    states(k, v, BEFORE, range(blocks))
    scatter(BEFORE)
    collect(AFTER)
    exchange(AFTER, range(half))

    @pl.when(group == half)
    def _():
        pl.semaphore_wait(higher_sem, groups - 1 - half)
        tell(higher_sem, at(half - 1, turned(half - 1, mine)))

    lax.fori_loop(0, 2, within, 0)
    exchange(AFTER, range(half, groups))
    collect(BEFORE)
    higher = jnp.where(group < half - 1, half - 1 - group, jnp.where(group == half - 1, 1, groups - 1 - group))

    @pl.when((group != half) & (group < groups - 1))
    def _():
        pl.semaphore_wait(higher_sem, higher)

    exchange(BEFORE, range(groups))

    @pl.when(group < half)
    def _():
        gather(BEFORE)
        exchange_sum(BEFORE)
        give_back(BEFORE)

    lax.fori_loop(2, blocks, within, 0)

    @pl.when(group >= half)
    def _():
        gather(AFTER)
        exchange_sum(AFTER)
        give_back(AFTER)

    @pl.when(group >= half)
    def _():
        gather(BEFORE)
        give_back(BEFORE)

    @pl.when(group < half)
    def _():
        gather(AFTER)
        give_back(AFTER)

    wait(early_carry.at[pl.ds(0, MEMBERS - 1)], recv_sem.at[BEFORE, 1])
    across(scale, (q, g), (0, 1), early_carry, early_inner, early_part, early)
    for way in (BEFORE, AFTER):
        for j in range(groups):

            @pl.when(direct(way, j) | summed(way, j))
            def _():
                wait(totals.at[way], far_send_sem.at[way, j])

        wait(own.at[way, pl.ds(0, MEMBERS - 1)], send_sem.at[way, 0])
        wait(back.at[way, pl.ds(0, MEMBERS - 1)], send_sem.at[way, 1])
    wait(carry.at[pl.ds(0, MEMBERS - 1)], recv_sem.at[AFTER, 1])


def final_kernel(scale, k, v, early, part, inner, carry, *rest):
    outs, (ready, early_sem, sem) = rest[:4], rest[4:]
    stores = [pltpu.make_async_copy(early.at[i], outs[i], early_sem.at[i]) for i in range(2)]
    for store in stores:
        store.start()

    def done(i, block):
        here = pl.ds(block * GROUP, GROUP)
        store = pltpu.make_async_copy(ready.at[i, here], outs[2 + i].at[here], sem.at[i, block])
        store.start()
        stores.append(store)

    across(scale, (v, k), (1, 0), carry, inner, part, ready, done)
    for store in stores:
        store.wait()


def shards(queries, keys, values, grad_out):
    rows, width = queries.shape
    blocks, heads = rows // GROUP, width // DH
    count = lax.axis_size("seq")
    groups = count // MEMBERS
    piece = heads * DH // MEMBERS
    scale = (DH * rows * count) ** (-0.5)
    anywhere = pl.BlockSpec(memory_space=pl.ANY)
    vmem = pl.BlockSpec(memory_space=pltpu.VMEM)
    f32 = jnp.float32
    array = pltpu.VMEM((rows, width), jnp.bfloat16)
    pair = pltpu.VMEM((2, rows, width), jnp.bfloat16)
    parts = pltpu.VMEM((2, rows, width), f32)
    inner = pltpu.VMEM((blocks, heads * DH, DH), f32)
    carry = pltpu.VMEM((MEMBERS, piece, DH), f32)
    pieces = pltpu.VMEM((2, MEMBERS, piece, DH), f32)
    dma = pltpu.SemaphoreType.DMA
    operands = [
        pltpu.with_memory_space_constraint(x, pltpu.HBM) for x in (queries, keys, values, grad_out)
    ]
    held = pl.pallas_call(
        functools.partial(carry_kernel, scale, groups),
        out_shape=(array, array, pair, parts, inner, carry),
        in_specs=[anywhere] * 4,
        out_specs=(vmem,) * 6,
        scratch_shapes=[
            array, array, parts, inner, carry, pltpu.VMEM((2, piece, DH), f32),
            pieces, pieces, pltpu.VMEM((2, piece, DH), f32), pltpu.VMEM((2, piece, DH), f32),
            pltpu.VMEM((2, groups, piece, DH), f32), pieces,
            dma((4,)), dma((2, 2)), dma((2, 2)), dma((2, groups)), dma((2, groups)),
            pltpu.SemaphoreType.REGULAR,
        ],
        compiler_params=pltpu.CompilerParams(
            collective_id=0, has_side_effects=True, vmem_limit_bytes=32 * 1024 * 1024
        ),
        name="scan_and_blocks",
    )(*operands)
    held = [pltpu.with_memory_space_constraint(x, pltpu.VMEM) for x in held]
    out = jax.ShapeDtypeStruct((rows, width), jnp.bfloat16)
    return pl.pallas_call(
        functools.partial(final_kernel, scale),
        out_shape=(out,) * 4,
        in_specs=[vmem] * 6,
        out_specs=(anywhere,) * 4,
        scratch_shapes=[pair, dma((2,)), dma((2, blocks))],
        compiler_params=pltpu.CompilerParams(vmem_limit_bytes=32 * 1024 * 1024),
        name="across_blocks",
    )(*held)


def solution(mesh):
    placed = (P("seq", "head"),) * 4
    return jax.shard_map(shards, mesh=mesh, in_specs=placed, out_specs=placed, check_vma=False)
```
